128 devices in a mesh: seq: 16 (over x_hi, y, core), gate: 8 (over z, x_lo).
Axes of the slice: x: 4 (x_hi: 2, x_lo: 2; x = x_hi * 2 + x_lo), y: 4, z: 4, core: 2. Of those that a mesh axis runs over, the one named last changes fastest.
Arguments:
- tokens: bfloat16 [16384, 2048], P(('seq', 'gate')), may hold values from -6 to 6
- cotangent: bfloat16 [16384, 2048], P(('seq', 'gate')), may hold values from -6 to 6
- start_state: float32 [16, 4096], P('seq', 'gate'), may hold values from -6 to 6
- slot_table: int32 [16], P('gate'), may hold values from -1 to 9, as said below
- norm_gains: float32 [2, 2048], replicated, may hold values from 0.5 to 1.5
- gain_first: float32 [2, 2048], replicated, may hold values from -320 to 320
- gain_second: float32 [2, 2048], replicated, may hold values from 8.192 to 131.072
- block_params: float32 [10, 8, 256], replicated
- block_first: float32 [10, 8, 256], replicated, may hold values from -1024 to 1024
- block_second: float32 [10, 8, 256], replicated, may hold values from 245.76 to 1966.08
- input_weights: float32 [2, 2048, 4096], P(None, 'seq', 'gate'), may hold values from -0.125 to 0.125
- input_first: float32 [2, 2048, 4096], P(None, 'seq', 'gate'), may hold values from -112 to 112
- input_second: float32 [2, 2048, 4096], P(None, 'seq', 'gate'), may hold values from 0.73728 to 11.79648
- output_weights: float32 [4096, 2048], P('gate', 'seq'), may hold values from -0.375 to 0.375
- output_first: float32 [4096, 2048], P('gate', 'seq'), may hold values from -112 to 112
- output_second: float32 [4096, 2048], P('gate', 'seq'), may hold values from 0.73728 to 11.79648
- gate_weights: float32 [2, 16, 256, 256], P(None, 'gate', 'seq'), may hold values from -0.375 to 0.375
- gate_first: float32 [2, 16, 256, 256], P(None, 'gate', 'seq'), may hold values from -32 to 32
- gate_second: float32 [2, 16, 256, 256], P(None, 'gate', 'seq'), may hold values from 0.08192 to 1.31072
- hidden_weights: float32 [2, 2048, 6144], P(None, 'seq', 'gate'), may hold values from -0.125 to 0.125
- hidden_first: float32 [2, 2048, 6144], P(None, 'seq', 'gate'), may hold values from -112 to 112
- hidden_second: float32 [2, 2048, 6144], P(None, 'seq', 'gate'), may hold values from 0.73728 to 11.79648
- down_weights: float32 [6144, 2048], P('gate', 'seq'), may hold values from -0.15625 to 0.15625
- down_first: float32 [6144, 2048], P('gate', 'seq'), may hold values from -160 to 160
- down_second: float32 [6144, 2048], P('gate', 'seq'), may hold values from 2.048 to 32.768
Outputs:
- layer_output: bfloat16 [16384, 2048], P(('seq', 'gate'))
- tokens_gradient: float32 [16384, 2048], P(('seq', 'gate'))
- gain_moment: float32 [2, 2048], replicated
- gain_square: float32 [2, 2048], replicated
- gain_master: float32 [2, 2048], replicated
- block_moment: float32 [10, 8, 256], replicated
- block_square: float32 [10, 8, 256], replicated
- block_master: float32 [10, 8, 256], replicated
- input_moment: float32 [2, 2048, 4096], P(None, 'seq', 'gate')
- input_square: float32 [2, 2048, 4096], P(None, 'seq', 'gate')
- input_master: float32 [2, 2048, 4096], P(None, 'seq', 'gate')
- output_moment: float32 [4096, 2048], P('gate', 'seq')
- output_square: float32 [4096, 2048], P('gate', 'seq')
- output_master: float32 [4096, 2048], P('gate', 'seq')
- gate_moment: float32 [2, 16, 256, 256], P(None, 'gate', 'seq')
- gate_square: float32 [2, 16, 256, 256], P(None, 'gate', 'seq')
- gate_master: float32 [2, 16, 256, 256], P(None, 'gate', 'seq')
- hidden_moment: float32 [2, 2048, 6144], P(None, 'seq', 'gate')
- hidden_square: float32 [2, 2048, 6144], P(None, 'seq', 'gate')
- hidden_master: float32 [2, 2048, 6144], P(None, 'seq', 'gate')
- down_moment: float32 [6144, 2048], P('gate', 'seq')
- down_square: float32 [6144, 2048], P('gate', 'seq')
- down_master: float32 [6144, 2048], P('gate', 'seq')
The draws below stay inside these ranges and needn't reach their ends.
Inputs may be any that keep to these rules, and one draw needn't show every extreme that they name: `slot_table`: each of the 10 block numbers stands in exactly one slot; slots 2 * g onward belong to index g of gate, which holds one or two live slots, the live ones first in its range.
All inputs are finite; a program needn't handle non-finite values.
Results may differ from the reference program's by a relative error of at most 0.028.
Values may be sent and summed in bfloat16 or wider, within the bound.
No kernel may reach another device: no remote copies, remote signals or barrier semaphores. Data moves between devices by JAX's collectives and lax.ppermute only.
A program may use at most 192 MiB of HBM per device.

```python
import math
import jax
import jax.numpy as jnp
from jax import lax

D = 2048
FF = 6144
NBLK = 10
BLOCK = 256
KERNEL = 4
STEP = 10
SEQ_LEN = 1024
SLOTS = 2
PSLOTS = 16
PW = 4096
TOKENS = 16384
N_SEQ = 16


def draw_slot_table(key, part):
    key = jax.random.fold_in(key, 11)
    devices = PSLOTS // SLOTS
    base_count = NBLK // devices
    extra_count = NBLK - base_count * devices
    device_key, block_key = jax.random.split(key)
    device_order = jax.random.permutation(device_key, devices)
    counts = base_count + (device_order < extra_count).astype(jnp.int32)
    slot_index = jnp.arange(PSLOTS, dtype=jnp.int32) % SLOTS
    device_of = jnp.arange(PSLOTS, dtype=jnp.int32) // SLOTS
    live = slot_index < counts[device_of]
    position = jnp.cumsum(live.astype(jnp.int32)) - 1
    blocks = jax.random.permutation(block_key, NBLK).astype(jnp.int32)
    table = jnp.where(live, blocks[jnp.clip(position, 0, NBLK - 1)], -1)
    return table.astype(jnp.int32)


def draw_block_params(key, part):
    key = jax.random.fold_in(key, 23)
    keys = jax.random.split(key, 4)
    low_end = 0.2 / SEQ_LEN
    high_end = 0.006 + 0.2 / SEQ_LEN
    fraction = jax.random.uniform(keys[0], (NBLK, 1, BLOCK), jnp.float32)
    rate = low_end * (high_end / low_end) ** fraction
    decay_param = -jnp.log(jnp.expm1(rate))
    gate_bias = jax.random.uniform(keys[1], (NBLK, 2, BLOCK), jnp.float32, -1.0, 1.0)
    tap_weights = 0.5 * jax.random.normal(keys[2], (NBLK, KERNEL, BLOCK), jnp.float32)
    tap_bias = 0.3 * jax.random.normal(keys[3], (NBLK, 1, BLOCK), jnp.float32)
    return jnp.concatenate([decay_param, gate_bias, tap_weights, tap_bias], axis=1).astype(jnp.float32)


def level_of(rng, shape, cuts, low, largest):
    factor_of = 1.0
    for axis_at, parts in cuts:
        steps = jax.random.uniform(jax.random.fold_in(jax.random.fold_in(rng, 6), axis_at), (parts,), jnp.float32, low / len(cuts), largest / len(cuts))
        factor_of = factor_of * jnp.repeat(jnp.exp(steps), shape[axis_at] // parts).reshape((-1,) + (1,) * (len(shape) - 1 - axis_at))
    return factor_of


def noise(stream_key, extent, scale, limit, pieces=(), kind=jnp.bfloat16):
    result = scale * jax.random.normal(stream_key, extent, jnp.float32)
    if pieces:
        result = result * level_of(stream_key, extent, pieces, -0.22, 0.18)
    return jnp.clip(result, -limit, limit).astype(kind)


def setup_inputs(seed: int = 0) -> dict:
    splits = jax.random.split(jax.random.key(seed), 26)
    tokens = noise(splits[0], (TOKENS, D), 1.0, 6.0, ((0, 128),))
    cotangent = noise(splits[1], (TOKENS, D), 1.0, 6.0, ((0, 128),))
    start_state = noise(splits[2], (N_SEQ, PW), 1.0, 6.0, ((0, 16), (1, 8)), jnp.float32)
    slot_table = draw_slot_table(jax.random.fold_in(splits[25], 71), 0)
    norm_gains = jnp.clip(1.0 + 0.1 * jax.random.normal(splits[4], (2, D), jnp.float32), 0.5, 1.5)
    gain_first = noise(splits[5], (2, D), (0.45 * TOKENS ** 0.5), 320.0, (), jnp.float32)
    gain_second = jnp.clip(jnp.exp(jax.random.uniform(splits[6], (2, D), jnp.float32, math.log(8.192), math.log(131.072))), 8.192, 131.072)
    block_params = draw_block_params(jax.random.fold_in(splits[25], 71), 0)
    block_first = noise(splits[8], (NBLK, KERNEL + 4, BLOCK), (1.5 * TOKENS ** 0.5), 1024.0, (), jnp.float32)
    block_second = jnp.clip(jnp.exp(jax.random.uniform(splits[9], (NBLK, KERNEL + 4, BLOCK), jnp.float32, math.log(245.76), math.log(1966.08))), 245.76, 1966.08)
    input_weights = noise(splits[10], (2, D, PW), D ** -0.5, 0.125, ((1, 16), (2, 8)), jnp.float32)
    input_first = noise(splits[11], (2, D, PW), (0.45 * (0.09 * TOKENS) ** 0.5), 112.0, ((1, 16), (2, 8)), jnp.float32)
    input_second = jnp.clip(jnp.exp(math.log(11.79648) - 2.7725887 * jax.random.uniform(splits[12], (2, D, PW), jnp.float32) ** level_of(splits[12], (2, D, PW), ((1, 16), (2, 8)), -0.2, 0.2)), 0.73728, 11.79648)
    output_weights = noise(splits[13], (PW, D), (NBLK * BLOCK // 10) ** -0.5, 0.375, ((0, 8), (1, 16)), jnp.float32)
    output_first = noise(splits[14], (PW, D), (0.45 * (0.09 * TOKENS) ** 0.5), 112.0, ((0, 8), (1, 16)), jnp.float32)
    output_second = jnp.clip(jnp.exp(math.log(11.79648) - 2.7725887 * jax.random.uniform(splits[15], (PW, D), jnp.float32) ** level_of(splits[15], (PW, D), ((0, 8), (1, 16)), -0.2, 0.2)), 0.73728, 11.79648)
    gate_weights = noise(splits[16], (2, PSLOTS, BLOCK, BLOCK), BLOCK ** -0.5, 0.375, ((1, 8), (2, 16)), jnp.float32)
    gate_first = noise(splits[17], (2, PSLOTS, BLOCK, BLOCK), (0.045 * TOKENS ** 0.5), 32.0, ((1, 8), (2, 16)), jnp.float32)
    gate_second = jnp.clip(jnp.exp(math.log(1.31072) - 2.7725887 * jax.random.uniform(splits[18], (2, PSLOTS, BLOCK, BLOCK), jnp.float32) ** level_of(splits[18], (2, PSLOTS, BLOCK, BLOCK), ((1, 8), (2, 16)), -0.2, 0.2)), 0.08192, 1.31072)
    hidden_weights = noise(splits[19], (2, D, FF), D ** -0.5, 0.125, ((1, 16), (2, 8)), jnp.float32)
    hidden_first = noise(splits[20], (2, D, FF), (0.45 * (0.09 * TOKENS) ** 0.5), 112.0, ((1, 16), (2, 8)), jnp.float32)
    hidden_second = jnp.clip(jnp.exp(math.log(11.79648) - 2.7725887 * jax.random.uniform(splits[21], (2, D, FF), jnp.float32) ** level_of(splits[21], (2, D, FF), ((1, 16), (2, 8)), -0.2, 0.2)), 0.73728, 11.79648)
    down_weights = noise(splits[22], (FF, D), (FF // 4) ** -0.5, 0.15625, ((0, 8), (1, 16)), jnp.float32)
    down_first = noise(splits[23], (FF, D), (0.225 * TOKENS ** 0.5), 160.0, ((0, 8), (1, 16)), jnp.float32)
    down_second = jnp.clip(jnp.exp(math.log(32.768) - 2.7725887 * jax.random.uniform(splits[24], (FF, D), jnp.float32) ** level_of(splits[24], (FF, D), ((0, 8), (1, 16)), -0.2, 0.2)), 2.048, 32.768)
    return {"tokens": tokens, "cotangent": cotangent, "start_state": start_state, "slot_table": slot_table, "norm_gains": norm_gains, "gain_first": gain_first, "gain_second": gain_second, "block_params": block_params, "block_first": block_first, "block_second": block_second, "input_weights": input_weights, "input_first": input_first, "input_second": input_second, "output_weights": output_weights, "output_first": output_first, "output_second": output_second, "gate_weights": gate_weights, "gate_first": gate_first, "gate_second": gate_second, "hidden_weights": hidden_weights, "hidden_first": hidden_first, "hidden_second": hidden_second, "down_weights": down_weights, "down_first": down_first, "down_second": down_second}


@jax.custom_vjp
def low(v):
    return lax.optimization_barrier(v.astype(jnp.bfloat16)).astype(jnp.float32)

@jax.custom_vjp
def low_back(v):
    return v

def low_keep(v):
    return (low(v), None)

def low_pass(kept, grad):
    return (grad,)

def back_keep(v):
    return (v, None)

def back_low(kept, grad):
    return (low(grad),)
low.defvjp(low_keep, low_pass)
low_back.defvjp(back_keep, back_low)
NORM_EPS = 1e-06
BETA_ONE = 0.9
BETA_TWO = 0.999
ADAM_EPS = 1e-08
MATRIX_RATE = 0.02
SMALL_RATE = 0.2
VECTOR_RATE = 0.8
MATRIX_DECAY = 0.1
HIGHEST = lax.Precision.HIGHEST

def matmul(left_side, right_side):
    return jnp.dot(left_side, right_side, precision=HIGHEST, preferred_element_type=jnp.float32)

def scale_norm(values, gain):
    return values * lax.rsqrt(lax.optimization_barrier(jnp.mean(values * values, axis=-1, keepdims=True)) + NORM_EPS) * gain

def causal_taps(values, tap_weights, tap_bias):
    length = values.shape[0]
    padded = jnp.concatenate([jnp.zeros((KERNEL - 1, values.shape[1]), jnp.float32), values], axis=0)
    running = jnp.zeros_like(values) + tap_bias
    for offset in range(KERNEL):
        running = running + tap_weights[offset] * padded[KERNEL - 1 - offset:KERNEL - 1 - offset + length]
    return running

def gating(gate_a, gate_i, filtered, decay_param):
    log_rate = -8.0 * jax.nn.sigmoid(gate_a) * jax.nn.softplus(-decay_param)
    decays = jnp.exp(log_rate)
    drives = jnp.sqrt(-jnp.expm1(2.0 * log_rate)) * jax.nn.sigmoid(gate_i) * filtered
    return (decays, drives)

def sequence_forward(values, initial, weights, vectors, column_mask):
    gains, input_w, output_w, gate_w, hidden_w, down_w = weights
    length = values.shape[0]
    normed = low(scale_norm(values, gains[0]))
    branch_x = low_back(matmul(normed, input_w[0]))
    branch_y = low_back(matmul(normed, input_w[1]))
    filtered = causal_taps(branch_x, vectors[3:3 + KERNEL], vectors[3 + KERNEL])
    filtered_low = low(filtered).reshape(length, PSLOTS, BLOCK)
    gate_a = low_back(jnp.einsum('lsc,scd->lsd', filtered_low, gate_w[0], precision=HIGHEST).reshape(length, PW)) + vectors[1]
    gate_i = low_back(jnp.einsum('lsc,scd->lsd', filtered_low, gate_w[1], precision=HIGHEST).reshape(length, PW)) + vectors[2]
    decays, drives = gating(gate_a, gate_i, filtered, vectors[0])

    def advance(state, inputs_pair):
        state = inputs_pair[0] * state + inputs_pair[1]
        return (state, state)
    _, states = lax.scan(advance, initial, (decays, drives))
    mixed = low(states * jax.nn.gelu(branch_y) * column_mask)
    middle = values + low_back(matmul(mixed, output_w))
    second = low(scale_norm(middle, gains[1]))
    gate_value = low_back(matmul(second, hidden_w[0]))
    up_value = low_back(matmul(second, hidden_w[1]))
    hidden = low(jax.nn.gelu(gate_value) * up_value)
    return middle + matmul(hidden, down_w)

def adamw(weight, gradient, first_moment, second_moment, step_rate, decay_rate):
    moment = BETA_ONE * first_moment + (1.0 - BETA_ONE) * gradient
    square = BETA_TWO * second_moment + (1.0 - BETA_TWO) * gradient * gradient
    fix_one = 1.0 - BETA_ONE ** STEP
    fix_two = 1.0 - BETA_TWO ** STEP
    master = weight - step_rate * (moment / fix_one / (jnp.sqrt(square / fix_two) + ADAM_EPS) + decay_rate * weight)
    return (moment, square, master)

def reference(tokens, cotangent, start_state, slot_table, norm_gains, gain_first, gain_second, block_params, block_first, block_second, input_weights, input_first, input_second, output_weights, output_first, output_second, gate_weights, gate_first, gate_second, hidden_weights, hidden_first, hidden_second, down_weights, down_first, down_second):
    column_mask = jnp.repeat((slot_table >= 0).astype(jnp.float32), BLOCK)
    select = (slot_table[:, None] == jnp.arange(NBLK, dtype=jnp.int32)[None, :]).astype(jnp.float32)

    def forward(values, gains, params, input_w, output_w, gate_w, hidden_w, down_w):
        vectors = jnp.einsum('sb,bkc->ksc', select, params, precision=HIGHEST).reshape(KERNEL + 4, PW)
        weights = (gains, low(input_w), low(output_w), low(gate_w), low(hidden_w), low(down_w))
        runner = jax.checkpoint(lambda inputs_pair: sequence_forward(inputs_pair[0], inputs_pair[1], weights, vectors, column_mask))
        outputs = lax.map(runner, (values.reshape(N_SEQ, SEQ_LEN, D), start_state))
        return outputs.reshape(TOKENS, D)
    primals = (tokens.astype(jnp.float32), norm_gains, block_params, input_weights, output_weights, gate_weights, hidden_weights, down_weights)
    output, pullback = jax.vjp(forward, *primals)
    gradients = pullback(cotangent.astype(jnp.float32))
    gain_moment, gain_square, gain_master = adamw(norm_gains, gradients[1], gain_first, gain_second, SMALL_RATE, 0.0)
    block_moment, block_square, block_master = adamw(block_params, gradients[2], block_first, block_second, VECTOR_RATE, 0.0)
    input_moment, input_square, input_master = adamw(input_weights, gradients[3], input_first, input_second, MATRIX_RATE, MATRIX_DECAY)
    output_moment, output_square, output_master = adamw(output_weights, gradients[4], output_first, output_second, MATRIX_RATE, MATRIX_DECAY)
    gate_moment, gate_square, gate_master = adamw(gate_weights, gradients[5], gate_first, gate_second, MATRIX_RATE, MATRIX_DECAY)
    hidden_moment, hidden_square, hidden_master = adamw(hidden_weights, gradients[6], hidden_first, hidden_second, MATRIX_RATE, MATRIX_DECAY)
    down_moment, down_square, down_master = adamw(down_weights, gradients[7], down_first, down_second, MATRIX_RATE, MATRIX_DECAY)
    return (output.astype(jnp.bfloat16), gradients[0], gain_moment, gain_square, gain_master, block_moment, block_square, block_master, input_moment, input_square, input_master, output_moment, output_square, output_master, gate_moment, gate_square, gate_master, hidden_moment, hidden_square, hidden_master, down_moment, down_square, down_master)
```

```python
import functools

import jax
import jax.numpy as jnp
from jax import lax
from jax.experimental import pallas as pl
from jax.experimental.pallas import tpu as pltpu
from jax.sharding import PartitionSpec as P

NBLK = 10
BLOCK = 256
KERNEL = 4
STEP = 10

NORM_EPS = 1e-06
BETA_ONE = 0.9
BETA_TWO = 0.999
ADAM_EPS = 1e-08
MATRIX_RATE = 0.02
SMALL_RATE = 0.2
VECTOR_RATE = 0.8
MATRIX_DECAY = 0.1
HIGHEST = lax.Precision.HIGHEST

RING = 4
GROUP = 2 * RING
TILE = 8
LANES = 128
PIECES = 12
VMEM = 56 * 1024 * 1024

BF16 = jnp.bfloat16
F32 = jnp.float32


def move(value, axis, step):
    size = lax.axis_size(axis)
    return lax.ppermute(value, axis, [(k, (k + step) % size) for k in range(size)])


def across(value):
    return move(value, "x", 1)


def up(value):
    return move(value, "z", 1)


def down(value):
    return move(value, "z", -1)


def plus(*terms):
    total = terms[0].astype(F32)
    for term in terms[1:]:
        total = total + term.astype(F32)
    return total


def plus_low(*terms):
    return plus(*terms).astype(BF16)


def after(value, *others):
    return lax.optimization_barrier((value, *others))[0]


def gather(value):
    half = value.shape[0] // 2
    a, b = value[:half], value[half:]
    a_x = across(a)
    below, above = up(value), down(value)
    b_x = across(b)
    ax_below, ax_above = up(a_x), down(a_x)
    far = up(below)
    bx_above, bx_below = across(above[half:]), across(below[half:])
    ax_far = down(ax_above)
    bx_far = across(far[half:])
    return [
        value, a_x, b_x,
        above, ax_above, bx_above,
        far, ax_far, bx_far,
        below, ax_below, bx_below,
    ]


def gather_rows(value, other, h):
    pair = jnp.stack([value, other])
    pair = jnp.where(h == 0, pair, pair[::-1])
    return lax.all_gather(pair, ("y", "c"), axis=0, tiled=False)


def scatter_rows(value):
    return lax.psum_scatter(value, ("y", "c"), scatter_dimension=0, tiled=False)


def halves(part, h):
    mine = lax.dynamic_index_in_dim(part, h, 0, keepdims=False)
    return mine, lax.dynamic_index_in_dim(part, 1 - h, 0, keepdims=False)


def trade(pieces):
    return lax.all_to_all(pieces, ("z", "x"), 0, 0)


def scatter(partial, beside=None):
    pieces = trade(partial.reshape(GROUP, -1, partial.shape[1]))
    if beside is not None:
        pieces, beside = lax.optimization_barrier((pieces, beside))
    return jnp.sum(pieces.astype(F32), axis=0), beside


def scatter_seq(mine, theirs):
    got = move(theirs, "c", 1)

    def block(dh, dy):
        return plus(mine[RING * dh + dy], got[RING * dh + dy])

    far_up = move(block(0, 2).astype(BF16), "y", 1)
    far_down = move(block(1, 2).astype(BF16), "y", -1)
    o_below = move(block(1, 1).astype(BF16), "y", 1)
    above = move(block(0, 3).astype(BF16), "y", -1)
    below = move(plus_low(block(0, 1), far_up), "y", 1)
    o_above = move(plus_low(block(1, 3), far_down), "y", -1)
    return plus(block(0, 0), below, above), plus_low(block(1, 0), o_below, o_above)


def sum_over(value, axes):
    for axis in axes:
        size = lax.axis_size(axis)
        step = 1
        while step < size:
            value = value + lax.ppermute(value, axis, [(k, k ^ step) for k in range(size)])
            step *= 2
    return value


def scale_norm(values, gain):
    return values * lax.rsqrt(jnp.mean(values * values, axis=-1, keepdims=True) + NORM_EPS) * gain


def norm_back(values, gain, d_normed):
    inverse = lax.rsqrt(jnp.mean(values * values, axis=-1, keepdims=True) + NORM_EPS)
    scaled = gain * d_normed
    d_values = inverse * scaled - values * inverse**3 * jnp.mean(
        scaled * values, axis=-1, keepdims=True
    )
    return d_values, inverse


def adamw(weight, gradient, first_moment, second_moment, step_rate, decay_rate):
    moment = BETA_ONE * first_moment + (1.0 - BETA_ONE) * gradient
    square = BETA_TWO * second_moment + (1.0 - BETA_TWO) * gradient * gradient
    fix_one = 1.0 - BETA_ONE**STEP
    fix_two = 1.0 - BETA_TWO**STEP
    master = weight - step_rate * (
        moment / fix_one / (jnp.sqrt(square / fix_two) + ADAM_EPS) + decay_rate * weight
    )
    return (moment, square, master)


GELU_SCALE = 0.7978845608028654
GELU_CUBE = 0.044715


def gelu_pair(y):
    t = jnp.tanh(GELU_SCALE * (y + GELU_CUBE * y * y * y))
    value = 0.5 * y * (1.0 + t)
    slope = 0.5 * (1.0 + t) + 0.5 * y * (1.0 - t * t) * GELU_SCALE * (
        1.0 + 3.0 * GELU_CUBE * y * y
    )
    return value, slope


def gelu(y):
    return 0.5 * y * (1.0 + jnp.tanh(GELU_SCALE * (y + GELU_CUBE * y * y * y)))


def one_minus_exp(v, exp_v):
    series = 1.0 + v * (1.0 / 7.0)
    for k in (6.0, 5.0, 4.0, 3.0, 2.0):
        series = 1.0 + v * (1.0 / k) * series
    return jnp.where(v > -0.5, -v * series, 1.0 - exp_v)


def shift_down(win, k):
    if k == 0:
        return win[TILE:]
    return pltpu.roll(win, k, 0)[TILE:]


def shift_up(win, k):
    return win[k : k + win.shape[0] - TILE]


def dot(left, right, dims):
    return lax.dot_general(left, right, (dims, ((), ())), preferred_element_type=F32)


def forward_gates(win, par_ref, gates):
    filtered = par_ref[7:8, :] + par_ref[3:4, :] * shift_down(win, 0)
    for k in range(1, KERNEL):
        filtered = filtered + par_ref[3 + k : 4 + k, :] * shift_down(win, k)
    low = filtered.astype(BF16)
    gate_a = dot(low, gates[0], ((1,), (0,))) + par_ref[1:2, :]
    gate_i = dot(low, gates[1], ((1,), (0,))) + par_ref[2:3, :]
    return filtered, low, jax.nn.sigmoid(gate_a), jax.nn.sigmoid(gate_i)


def unpack_gates(packed_ref, slot, gates, share):
    rows = share // 8
    for g in range(2):
        for half in range(2):
            for s in range(BLOCK // rows):
                at = pl.multiple_of(s * share + (4 * g + 2 * slot + half) * rows, rows)
                gates[g, s * rows : (s + 1) * rows, half * LANES : (half + 1) * LANES] = packed_ref[
                    pl.ds(at, rows), :
                ]


def fill_window(xs, branch_ref, order, chunk):
    xs[0:TILE, :] = jnp.zeros((TILE, xs.shape[1]), F32)

    @pl.loop(0, GROUP)
    def _(i):
        xs[pl.ds(TILE + i * chunk, chunk), :] = branch_ref[order[i], :, :BLOCK]


def scan_tile(a, b, rows):
    for s in (1, 2, 4):
        keep = rows >= s
        b = b + a * jnp.where(keep, pltpu.roll(b, s, 0), 0.0)
        a = a * jnp.where(keep, pltpu.roll(a, s, 0), 1.0)
    return a, b


def scan_tile_back(a, b, rows):
    for s in (1, 2, 4):
        keep = rows < TILE - s
        b = b + a * jnp.where(keep, pltpu.roll(b, TILE - s, 0), 0.0)
        a = a * jnp.where(keep, pltpu.roll(a, TILE - s, 0), 1.0)
    return a, b


def piece_copies(refs, whole, sems):
    copies, at = [], 0
    for k, ref in enumerate(refs):
        rows = ref.shape[0]
        copies.append(pltpu.make_async_copy(ref, whole.at[pl.ds(at, rows), :], sems.at[k]))
        at += rows
    return copies


def load_pieces(refs, whole, sems):
    copies = piece_copies(refs, whole, sems)
    for copy in copies:
        copy.start()
    for copy in copies:
        copy.wait()


def mix_steps(
    chunk, order, par_ref, branch_ref, gates, mixed_ref, mixed_rows, lanes, states_ref, xs
):
    fill_window(xs, branch_ref, order, chunk)
    rows = lax.broadcasted_iota(jnp.int32, (TILE, BLOCK), 0)

    def step(i, carry):
        at = pl.multiple_of(i * chunk, chunk)
        filtered, _, ra, ri = forward_gates(xs[pl.ds(at, chunk + TILE), :], par_ref, gates)
        log_rate = -8.0 * ra * par_ref[0:1, :]
        decay = jnp.exp(log_rate)
        drive = jnp.sqrt(one_minus_exp(2.0 * log_rate, decay * decay)) * ri * filtered
        tiles = []
        for k in range(chunk // TILE):
            part = slice(k * TILE, (k + 1) * TILE)
            a, b = scan_tile(decay[part], drive[part], rows)
            h = b + a * carry
            tiles.append(h)
            carry = jnp.broadcast_to(h[TILE - 1 : TILE], (TILE, BLOCK))
        states = jnp.concatenate(tiles, axis=0)
        states_ref[pl.ds(at, chunk), :] = states
        y = branch_ref[order[i], :, BLOCK:]
        mixed = (states * gelu(y) * par_ref[9:10, :]).astype(BF16)
        mixed_ref[order[i], :, lanes] = mixed
        mixed_rows[pl.ds(at, chunk), lanes] = mixed
        return carry

    lax.fori_loop(0, GROUP, step, jnp.broadcast_to(par_ref[10:11, :], (TILE, BLOCK)))


def mixer_kernel(chunk, share, order, par_ref, given_ref, *rest):
    pieces, rest = rest[:PIECES], rest[PIECES:]
    branch_ref, states_ref, mixed_ref, part_ref, all_ref, weights_ref = rest[:6]
    whole, weights, mixed_rows, gates, xs, sems, share_sems, out_sems = rest[6:]
    slot, slots = pl.program_id(0), pl.num_programs(0)
    width = slots * BLOCK

    def out_copies():
        return (
            pltpu.make_async_copy(whole, all_ref, out_sems.at[0]),
            pltpu.make_async_copy(weights, weights_ref, out_sems.at[1]),
        )

    @pl.when(slot == 0)
    def _():
        copies = piece_copies(pieces, whole, sems)
        for h in range(2):
            for k in range(GROUP):
                to = pl.ds((h * GROUP + k) * share, share)
                copies.append(
                    pltpu.make_async_copy(
                        given_ref.at[k, h], weights.at[to, :], share_sems.at[h * GROUP + k]
                    )
                )
        for copy in copies:
            copy.start()
        for copy in copies:
            copy.wait()
        for copy in out_copies():
            copy.start()

    @pl.loop(0, 2)
    def _(n):
        lanes = pl.ds(pl.multiple_of(n * BLOCK, BLOCK), BLOCK)
        at = pl.multiple_of((2 * slot + n) * BLOCK, BLOCK)
        product = dot(whole[...], weights[:, pl.ds(at, BLOCK)], ((1,), (0,)))
        branch_ref[:, :, lanes] = product.reshape(GROUP, chunk, BLOCK)

    unpack_gates(weights.at[:, pl.ds(3 * width, LANES)], slot, gates, share)
    lanes = pl.ds(pl.multiple_of(slot * BLOCK, BLOCK), BLOCK)
    mix_steps(
        chunk, order, par_ref, branch_ref, gates, mixed_ref, mixed_rows, lanes, states_ref, xs
    )

    @pl.when(slot == slots - 1)
    def _():
        @pl.loop(0, part_ref.shape[1] // BLOCK)
        def _(n):
            at = pl.multiple_of(n * BLOCK, BLOCK)
            product = dot(
                mixed_rows[...], weights[pl.ds(at, BLOCK), 2 * width : 3 * width], ((1,), (1,))
            )
            part_ref[:, pl.ds(at, BLOCK)] = product.astype(BF16)

        for copy in out_copies():
            copy.wait()


def factor_kernel(
    chunk, share, order, par_ref, packed_ref, branch_ref, states_ref,
    low_ref, decay_ref, open_ref, y_ref, a_ref, i_ref, f_ref, l_ref, gates, xs,
):
    fill_window(xs, branch_ref, order, chunk)
    unpack_gates(packed_ref, pl.program_id(0), gates, share)

    def step(i, before):
        at = pl.multiple_of(i * chunk, chunk)
        here = pl.ds(at, chunk)
        filtered, low, ra, ri = forward_gates(xs[pl.ds(at, chunk + TILE), :], par_ref, gates)
        low_ref[here, :] = low
        log_rate = -8.0 * ra * par_ref[0:1, :]
        decay = jnp.exp(log_rate)
        square = decay * decay
        drop = jnp.sqrt(one_minus_exp(2.0 * log_rate, square))
        decay_ref[here, :] = decay
        states = states_ref[here, :]
        previous = shift_down(jnp.concatenate([before, states], axis=0), 1)
        y = branch_ref[order[i], :, BLOCK:]
        value, slope = gelu_pair(y)
        mask = par_ref[9:10, :]
        open_ref[here, :] = (value * mask).astype(BF16)
        y_ref[here, :] = (states * slope * mask).astype(BF16)
        rate_pull = previous * decay - filtered * ri * square / drop
        pull_a = rate_pull * (-8.0 * par_ref[0:1, :]) * ra * (1.0 - ra)
        a_ref[here, :] = pull_a.astype(BF16)
        l_ref[here, :] = (rate_pull * (8.0 * par_ref[8:9, :]) * ra).astype(BF16)
        i_ref[here, :] = (drop * filtered * ri * (1.0 - ri)).astype(BF16)
        f_ref[here, :] = (drop * ri).astype(BF16)
        return states[chunk - TILE :]

    lax.fori_loop(0, GROUP, step, jnp.broadcast_to(par_ref[10:11, :], (TILE, BLOCK)))


def fold(value):
    return jnp.sum(value.reshape(-1, TILE, value.shape[-1]), axis=0)


def unmix_steps(
    chunk, order, par_ref, branch_ref, gates, d_mixed_ref,
    low_ref, decay_ref, open_ref, y_ref, a_ref, i_ref, f_ref, l_ref,
    d_branch_ref, d_rows, lanes_x, lanes_y, d_gate_ref, d_par_ref, ga, gi, sums,
):
    rows = lax.broadcasted_iota(jnp.int32, (TILE, BLOCK), 0)
    sums[...] = jnp.zeros_like(sums)

    def step(n, carries):
        carry, behind = carries
        i = GROUP - 1 - n
        at = pl.multiple_of(i * chunk, chunk)
        here = pl.ds(at, chunk)
        d_mixed = d_mixed_ref[order[i]]
        d_states = d_mixed * open_ref[here, :].astype(F32)
        d_y = (d_mixed * y_ref[here, :].astype(F32)).astype(BF16)
        d_branch_ref[order[i], :, lanes_y] = d_y
        d_rows[here, lanes_y] = d_y
        decay = decay_ref[here, :].astype(F32)
        pushed = decay * d_states
        tiles = [None] * (chunk // TILE)
        for k in reversed(range(chunk // TILE)):
            part = slice(k * TILE, (k + 1) * TILE)
            a, b = scan_tile_back(decay[part], pushed[part], rows)
            w = b + a * carry
            behind_w = jnp.where(rows < TILE - 1, pltpu.roll(w, TILE - 1, 0), carry)
            tiles[k] = d_states[part] + behind_w
            carry = jnp.broadcast_to(w[0:1], (TILE, BLOCK))
        carried = jnp.concatenate(tiles, axis=0)
        d_a = carried * a_ref[here, :].astype(F32)
        d_i = carried * i_ref[here, :].astype(F32)
        a_low, i_low = d_a.astype(BF16), d_i.astype(BF16)
        ga[here, :] = a_low
        gi[here, :] = i_low
        d_f = (
            carried * f_ref[here, :].astype(F32)
            + dot(a_low, gates[0], ((1,), (1,)))
            + dot(i_low, gates[1], ((1,), (1,)))
        )
        win = jnp.concatenate([d_f, behind], axis=0)
        x = branch_ref[order[i], :, :BLOCK]
        d_u = jnp.zeros((chunk, BLOCK), F32)
        for k in range(KERNEL):
            moved = shift_up(win, k)
            d_u = d_u + par_ref[3 + k : 4 + k, :] * moved
            sums[3 + k] += fold(moved * x)
        d_u = d_u.astype(BF16)
        d_branch_ref[order[i], :, lanes_x] = d_u
        d_rows[here, lanes_x] = d_u
        sums[0] += fold(carried * l_ref[here, :].astype(F32))
        sums[1] += fold(d_a)
        sums[2] += fold(d_i)
        sums[7] += fold(d_f)
        return carry, d_f[:TILE]

    nothing = jnp.zeros((TILE, BLOCK), F32)
    lax.fori_loop(0, GROUP, step, (nothing, nothing))
    d_gate_ref[0, 0] = dot(low_ref[...], ga[...], ((0,), (0,))).astype(BF16)
    d_gate_ref[1, 0] = dot(low_ref[...], gi[...], ((0,), (0,))).astype(BF16)
    for k in range(TILE):
        d_par_ref[k : k + 1, :] = jnp.sum(sums[k], axis=0, keepdims=True)


def unmixer_kernel(
    chunk, share, order, par_ref, packed_ref, weights_ref, output_ref, branch_ref,
    low_ref, decay_ref, open_ref, y_ref, a_ref, i_ref, f_ref, l_ref, *rest,
):
    pieces, rest = rest[:PIECES], rest[PIECES:]
    d_branch_ref, d_gate_ref, d_par_ref, part_ref, all_ref = rest[:5]

    def input_copy():
        lanes = pl.ds(0, input_ref.shape[1])
        return pltpu.make_async_copy(weights_ref.at[:, lanes], input_ref, input_sem)

    whole, input_ref, d_rows, d_mixed, gates, ga, gi, sums, sems, out_sem, input_sem = rest[5:]
    slot, slots = pl.program_id(0), pl.num_programs(0)

    @pl.when(slot == 0)
    def _():
        load_pieces(pieces, whole, sems)
        pltpu.make_async_copy(whole, all_ref, out_sem).start()
        input_copy().start()

    product = dot(whole[...], output_ref[...], ((1,), (0,)))
    d_mixed[...] = product.reshape(GROUP, chunk, BLOCK)

    unpack_gates(packed_ref, slot, gates, share)
    at_x = pl.multiple_of(slot * 2 * BLOCK, 2 * BLOCK)
    at_y = pl.multiple_of(slot * 2 * BLOCK + BLOCK, BLOCK)
    unmix_steps(
        chunk, order, par_ref, branch_ref, gates, d_mixed,
        low_ref, decay_ref, open_ref, y_ref, a_ref, i_ref, f_ref, l_ref,
        d_branch_ref, d_rows, pl.ds(at_x, BLOCK), pl.ds(at_y, BLOCK), d_gate_ref, d_par_ref,
        ga, gi, sums,
    )

    @pl.when(slot == slots - 1)
    def _():
        input_copy().wait()

        @pl.loop(0, part_ref.shape[1] // BLOCK)
        def _(n):
            at = pl.multiple_of(n * BLOCK, BLOCK)
            product = dot(d_rows[...], input_ref[pl.ds(at, BLOCK), :], ((1,), (1,)))
            part_ref[:, pl.ds(at, BLOCK)] = product.astype(BF16)

        pltpu.make_async_copy(whole, all_ref, out_sem).wait()


def in_h_order(block):
    lanes = block.shape[-1]
    return jnp.concatenate([block[:, h].reshape(-1, lanes) for h in range(2)], axis=0)


def pull_kernel(order, given_ref, down_ref, out_ref, all_ref, whole, sems, out_sem):
    step, steps = pl.program_id(0), pl.num_programs(0)
    chunk = given_ref.shape[1]

    @pl.when(step == 0)
    def _():
        copies = []
        for i in range(GROUP):
            to = pl.ds(pl.multiple_of(order[i] * chunk, chunk), chunk)
            copies.append(pltpu.make_async_copy(given_ref.at[i], whole.at[to, :], sems.at[i]))
        for copy in copies:
            copy.start()
        for copy in copies:
            copy.wait()
        pltpu.make_async_copy(whole, all_ref, out_sem).start()

    out_ref[...] = dot(whole[...], in_h_order(down_ref[...]), ((1,), (0,)))

    @pl.when(step == steps - 1)
    def _():
        pltpu.make_async_copy(whole, all_ref, out_sem).wait()


def feed_kernel(*rest):
    chunk_of, feed_ref, d_hidden_ref = rest[:3]
    pieces, rest = rest[3 : 3 + PIECES], rest[3 + PIECES :]
    hidden_ref, d_gate_ref, d_up_ref, part_ref, all_ref = rest[:5]
    whole, weights, d_both, gates, ups, sems, weight_sems, out_sem = rest[5:]
    step, steps = pl.program_id(0), pl.num_programs(0)
    tiles = weights.shape[1] // BLOCK
    rows = whole.shape[0] // GROUP

    share = feed_ref.shape[2]

    def weight_copies():
        for t in range(tiles // 2):
            for lanes in (pl.ds(t * BLOCK, BLOCK), pl.ds((t + tiles // 2) * BLOCK, BLOCK)):
                for h in range(2):
                    for k in range(GROUP):
                        to = pl.ds((h * GROUP + k) * share, share)
                        yield pltpu.make_async_copy(
                            feed_ref.at[k, h, :, lanes], weights.at[to, lanes], weight_sems.at[t]
                        )

    @pl.when(step == 0)
    def _():
        copies = piece_copies(pieces, whole, sems)
        for copy in copies:
            copy.start()
        for copy in weight_copies():
            copy.start()
        for copy in copies:
            copy.wait()
        pltpu.make_async_copy(whole, all_ref, out_sem).start()

    for t in range(tiles // 2):
        @pl.when(step == t)
        def _():
            both = 2 * BLOCK
            pltpu.make_async_copy(
                weights.at[:, pl.ds(0, both)], weights.at[:, pl.ds(0, both)], weight_sems.at[t]
            ).wait()

    at_gate = pl.multiple_of(step * BLOCK, BLOCK)
    at_up = pl.multiple_of((step + tiles // 2) * BLOCK, BLOCK)

    gates[...] = dot(whole[...], weights[:, pl.ds(at_gate, BLOCK)], ((1,), (0,)))
    ups[...] = dot(whole[...], weights[:, pl.ds(at_up, BLOCK)], ((1,), (0,)))

    @pl.loop(0, GROUP)
    def _(m):
        here = pl.ds(pl.multiple_of(m * rows, rows), rows)
        up_value = ups[here, :]
        value, slope = gelu_pair(gates[here, :])
        hidden_ref[here, :] = (value * up_value).astype(BF16)
        d_hidden = d_hidden_ref[here, :]
        d_gate = (d_hidden * up_value * slope).astype(BF16)
        d_up = (d_hidden * value).astype(BF16)
        d_gate_ref[here, :] = d_gate
        d_up_ref[here, :] = d_up
        to = pl.ds(pl.multiple_of(chunk_of[m] * rows, rows), rows)
        d_both[to, pl.ds(at_gate, BLOCK)] = d_gate
        d_both[to, pl.ds(at_up, BLOCK)] = d_up

    @pl.when(step == steps - 1)
    def _():
        @pl.loop(0, part_ref.shape[1] // BLOCK)
        def _(n):
            at = pl.multiple_of(n * BLOCK, BLOCK)
            product = dot(d_both[...], weights[pl.ds(at, BLOCK), :], ((1,), (1,)))
            part_ref[:, pl.ds(at, BLOCK)] = product.astype(BF16)

        pltpu.make_async_copy(whole, all_ref, out_sem).wait()


def down_kernel(order, hidden_ref, down_ref, part_ref, rows_ref):
    chunk = hidden_ref.shape[0] // GROUP

    @pl.when(pl.program_id(0) == 0)
    def _():
        for i in range(GROUP):
            at = pl.multiple_of(order[i] * chunk, chunk)
            rows_ref[i * chunk : (i + 1) * chunk, :] = hidden_ref[pl.ds(at, chunk), :]

    weights = down_ref[...].reshape(BLOCK, down_ref.shape[3])
    part_ref[...] = dot(rows_ref[...], weights, ((1,), (1,))).astype(BF16)


def feed_grad_kernel(second_ref, cotangent_ref, d_gate_ref, d_up_ref, hidden_ref, out_ref):
    ff = hidden_ref.shape[1]
    shape = out_ref.shape[:3] + (ff,)
    left = second_ref[...].T
    for k, ref in enumerate((d_gate_ref, d_up_ref)):
        product = dot(left, ref[...], ((1,), (0,)))
        out_ref[:, :, :, k * ff : (k + 1) * ff] = product.astype(BF16).reshape(shape)
    product = dot(cotangent_ref[...].T, hidden_ref[...], ((1,), (0,)))
    out_ref[:, :, :, 2 * ff :] = product.astype(BF16).reshape(shape)


def split_twins(value, core, mine_ref, theirs_ref, lanes):
    half = value.shape[0] // 2
    top, bottom = value[:half].astype(BF16), value[half:].astype(BF16)
    mine_ref[0, :, lanes] = jnp.where(core == 0, top, bottom)
    theirs_ref[0, :, lanes] = jnp.where(core == 0, bottom, top)


def mixer_grad_kernel(
    place, left_ref, right_ref, out_ref, mixed_ref, weight_ref, d_gate_ref,
    mine_ref, theirs_ref, gain_ref,
):
    core, pair = place[GROUP], place[pl.program_id(0)]
    product = dot(left_ref[...].T, right_ref[...], ((1,), (0,)))
    width = product.shape[1]
    split_twins(product, core, mine_ref, theirs_ref, slice(0, width))
    scaled = product * weight_ref[...].astype(F32)
    folded = scaled[:, :LANES]
    for k in range(1, width // LANES):
        folded = folded + scaled[:, k * LANES : (k + 1) * LANES]
    gain_ref[...] = folded
    product = dot(out_ref[...].T, mixed_ref[...], ((1,), (0,)))
    last = width + product.shape[1]
    split_twins(product, core, mine_ref, theirs_ref, slice(width, last))
    slots = d_gate_ref.shape[1]
    rows = product.shape[0] // 2 // 8
    for g in range(2):
        for j in range(slots):
            for half in range(2):
                at = (4 * g + 2 * j + half) * rows
                lanes = slice(half * LANES, (half + 1) * LANES)
                for ref, twin in ((mine_ref, core), (theirs_ref, 1 - core)):
                    start = pl.multiple_of((2 * pair + twin) * rows, rows)
                    ref[0, at : at + rows, last:] = d_gate_ref[g, j, pl.ds(start, rows), lanes]


def mixer_rows_kernel(input_ref, output_ref, gate_ref, out_ref):
    slots = gate_ref.shape[1]
    rows = gate_ref.shape[2]
    for j in range(slots):
        for k in range(2):
            at = (2 * j + k) * BLOCK
            part = input_ref[k, :, j * BLOCK : (j + 1) * BLOCK]
            out_ref[:, at : at + BLOCK] = part.astype(BF16)
    at = 2 * slots * BLOCK
    columns = slots * BLOCK
    out_ref[:, at : at + columns] = output_ref[...].T.astype(BF16)
    at += columns
    for g in range(2):
        for j in range(slots):
            for half in range(2):
                k = (4 * g + 2 * j + half) * rows
                part = gate_ref[g, j, :, half * LANES : (half + 1) * LANES]
                out_ref[k : k + rows, at:] = part.astype(BF16)


def feed_rows_kernel(hidden_ref, down_ref, out_ref):
    ff = hidden_ref.shape[2]
    for k in range(2):
        out_ref[:, k * ff : (k + 1) * ff] = hidden_ref[k].astype(BF16)
    out_ref[:, 2 * ff :] = down_ref[...].T.astype(BF16)


def mixer_adam_kernel(in_ref, *rest):
    given, made = rest[:9], rest[9:]
    slots, rows = given[6].shape[1], given[6].shape[2]
    for j in range(slots):
        lanes = slice(j * BLOCK, (j + 1) * BLOCK)
        for k in range(2):
            at = (2 * j + k) * BLOCK
            grad = in_ref[:, at : at + BLOCK]
            for ref, value in zip(made[:3], step_of(given[:3], grad, (k, slice(None), lanes))):
                ref[k, :, lanes] = value
        at = 2 * slots * BLOCK + j * BLOCK
        grad = in_ref[:, at : at + BLOCK].T
        for ref, value in zip(made[3:6], step_of(given[3:6], grad, (lanes,))):
            ref[lanes, :] = value
    at = 3 * slots * BLOCK
    for g in range(2):
        for j in range(slots):
            for half in range(2):
                k = (4 * g + 2 * j + half) * rows
                lanes = slice(half * LANES, (half + 1) * LANES)
                grad = in_ref[k : k + rows, at:]
                for ref, value in zip(made[6:], step_of(given[6:], grad, (g, j, slice(None), lanes))):
                    ref[g, j, :, lanes] = value


def feed_adam_kernel(grad_ref, *rest):
    given, made = rest[:6], rest[6:]
    ff = given[0].shape[2]
    for k in range(2):
        for t in range(ff // BLOCK):
            lanes = slice(t * BLOCK, (t + 1) * BLOCK)
            grad = grad_ref[:, k * ff + t * BLOCK : k * ff + (t + 1) * BLOCK].astype(F32)
            for ref, value in zip(made[:3], step_of(given[:3], grad, (k, slice(None), lanes))):
                ref[k, :, lanes] = value
    for t in range(ff // BLOCK):
        lanes = slice(t * BLOCK, (t + 1) * BLOCK)
        grad = grad_ref[:, 2 * ff + t * BLOCK : 2 * ff + (t + 1) * BLOCK].astype(F32).T
        for ref, value in zip(made[3:], step_of(given[3:], grad, (lanes,))):
            ref[lanes, :] = value


def step_of(refs, grad, at):
    return adamw(refs[0][at], grad, refs[1][at], refs[2][at], MATRIX_RATE, MATRIX_DECAY)


def kernel_call(body, name, out_shape, flops=0, moved=0, **options):
    return pl.pallas_call(
        body,
        out_shape=out_shape,
        compiler_params=pltpu.CompilerParams(vmem_limit_bytes=VMEM),
        cost_estimate=pl.CostEstimate(flops=flops, bytes_accessed=moved, transcendentals=0),
        name=name,
        **options,
    )


ANY = pl.BlockSpec(memory_space=pl.ANY)


def all_at(shape):
    return pl.BlockSpec(shape, lambda *_: (0,) * len(shape))


def recurrence_calls(chunk, slots, width, share):
    length, columns = GROUP * chunk, slots * BLOCK
    scalars = pl.BlockSpec(memory_space=pltpu.SMEM)
    par = pl.BlockSpec((16, BLOCK), lambda j: (0, j))
    branch = pl.BlockSpec((GROUP, chunk, 2 * BLOCK), lambda j: (0, 0, j))
    packed = pl.BlockSpec((width, LANES), lambda j: (0, 3 * columns // LANES))
    flat = pl.BlockSpec((length, BLOCK), lambda j: (0, j))
    flat_type = jax.ShapeDtypeStruct((length, columns), F32)
    flat_low = jax.ShapeDtypeStruct((length, columns), BF16)
    window = pltpu.VMEM((length + TILE, BLOCK), F32)
    gates = pltpu.VMEM((2, BLOCK, BLOCK), BF16)
    rows_type = jax.ShapeDtypeStruct((length, width), BF16)
    whole = pltpu.VMEM((length, width), BF16)
    size = length * columns

    mixer = kernel_call(
        functools.partial(mixer_kernel, chunk, share),
        "mix",
        [
            jax.ShapeDtypeStruct((GROUP, chunk, 2 * columns), F32),
            flat_type,
            jax.ShapeDtypeStruct((GROUP, chunk, columns), BF16),
            rows_type,
            rows_type,
            jax.ShapeDtypeStruct((width, 3 * columns + LANES), BF16),
        ],
        flops=6 * length * width * columns + 40 * size,
        moved=4 * length * width + 20 * size,
        grid=(slots,),
        in_specs=[scalars, par] + [ANY] * (1 + PIECES),
        out_specs=[
            branch,
            flat,
            all_at((GROUP, chunk, columns)),
            all_at((length, width)),
            ANY,
            ANY,
        ],
        scratch_shapes=[
            whole,
            pltpu.VMEM((width, 3 * columns + LANES), BF16),
            pltpu.VMEM((length, columns), BF16),
            gates,
            window,
            pltpu.SemaphoreType.DMA((PIECES,)),
            pltpu.SemaphoreType.DMA((16,)),
            pltpu.SemaphoreType.DMA((2,)),
        ],
    )
    factors = kernel_call(
        functools.partial(factor_kernel, chunk, share),
        "factors",
        [flat_low, flat_type] + [flat_low] * 6,
        flops=60 * size,
        moved=44 * size,
        grid=(slots,),
        in_specs=[scalars, par, packed, branch, flat],
        out_specs=[flat] * 8,
        scratch_shapes=[gates, window],
    )
    unmixer = kernel_call(
        functools.partial(unmixer_kernel, chunk, share),
        "unmix",
        [
            jax.ShapeDtypeStruct((GROUP, chunk, 2 * columns), BF16),
            jax.ShapeDtypeStruct((2, slots, BLOCK, BLOCK), BF16),
            jax.ShapeDtypeStruct((TILE, columns), F32),
            rows_type,
            rows_type,
        ],
        flops=6 * length * width * columns + 40 * size,
        moved=4 * length * width + 44 * size,
        grid=(slots,),
        in_specs=[
            scalars,
            par,
            packed,
            ANY,
            pl.BlockSpec((width, BLOCK), lambda j: (0, 2 * slots + j)),
            branch,
        ]
        + [flat] * 8
        + [ANY] * PIECES,
        out_specs=[
            all_at((GROUP, chunk, 2 * columns)),
            pl.BlockSpec((2, 1, BLOCK, BLOCK), lambda j: (0, j, 0, 0)),
            pl.BlockSpec((TILE, BLOCK), lambda j: (0, j)),
            all_at((length, width)),
            ANY,
        ],
        scratch_shapes=[
            whole,
            pltpu.VMEM((width, 2 * columns), BF16),
            pltpu.VMEM((length, 2 * columns), BF16),
            pltpu.VMEM((GROUP, chunk, BLOCK), F32),
            gates,
            pltpu.VMEM((length, BLOCK), BF16),
            pltpu.VMEM((length, BLOCK), BF16),
            pltpu.VMEM((TILE, TILE, BLOCK), F32),
            pltpu.SemaphoreType.DMA((PIECES,)),
            pltpu.SemaphoreType.DMA,
            pltpu.SemaphoreType.DMA,
        ],
    )
    return mixer, factors, unmixer


def feed_calls(length, width, share, ff):
    rows_type = jax.ShapeDtypeStruct((length, width), BF16)
    units = jax.ShapeDtypeStruct((length, ff), BF16)
    whole = pltpu.VMEM((length, width), BF16)
    tiles = ff // BLOCK
    unit = pl.BlockSpec((length, BLOCK), lambda t: (0, t))
    sems = [pltpu.SemaphoreType.DMA((PIECES,)), pltpu.SemaphoreType.DMA]
    work = 2 * length * width * ff
    half = width // (2 * share)
    pull = kernel_call(
        pull_kernel,
        "pull",
        [jax.ShapeDtypeStruct((length, ff), F32), rows_type],
        flops=work,
        moved=8 * length * width,
        grid=(tiles,),
        in_specs=[
            pl.BlockSpec(memory_space=pltpu.SMEM),
            ANY,
            pl.BlockSpec((GROUP, 2, share, BLOCK), lambda t: (0, 0, 0, 2 * tiles + t)),
        ],
        out_specs=[unit, ANY],
        scratch_shapes=[whole] + sems,
    )
    feed = kernel_call(
        feed_kernel,
        "feed",
        [units, units, units, rows_type, rows_type],
        flops=4 * work,
        moved=10 * length * width,
        grid=(tiles,),
        in_specs=[pl.BlockSpec(memory_space=pltpu.SMEM), ANY, unit] + [ANY] * PIECES,
        out_specs=[unit, unit, unit, all_at((length, width)), ANY],
        scratch_shapes=[
            whole,
            pltpu.VMEM((width, 2 * ff), BF16),
            pltpu.VMEM((length, 2 * ff), BF16),
            pltpu.VMEM((length, BLOCK), F32),
            pltpu.VMEM((length, BLOCK), F32),
            sems[0],
            pltpu.SemaphoreType.DMA((tiles,)),
            sems[1],
        ],
    )
    down_call = kernel_call(
        down_kernel,
        "down",
        rows_type,
        flops=work,
        moved=4 * length * width,
        grid=(width // BLOCK,),
        in_specs=[
            pl.BlockSpec(memory_space=pltpu.SMEM),
            all_at((length, ff)),
            pl.BlockSpec(
                (BLOCK // share, 1, share, ff), lambda n: (n % (half // 2), n // (half // 2), 0, 2)
            ),
        ],
        out_specs=pl.BlockSpec((length, BLOCK), lambda n: (0, n)),
        scratch_shapes=[pltpu.VMEM((length, ff), BF16)],
    )
    grads = kernel_call(
        feed_grad_kernel,
        "feed_grads",
        jax.ShapeDtypeStruct((half, 2, share, 3 * ff), BF16),
        flops=3 * work,
        moved=10 * length * width,
        grid=(width // (2 * BLOCK),),
        in_specs=[pl.BlockSpec((length, 2 * BLOCK), lambda n: (0, n))] * 2
        + [all_at((length, ff))] * 3,
        out_specs=pl.BlockSpec(
            (2 * BLOCK // share, 1, share, 3 * ff),
            lambda n: (n % (half // 4), n // (half // 4), 0, 0),
        ),
    )
    return pull, feed, down_call, grads


def mixer_grad_call(length, width, columns, slots):
    pairs = width // BLOCK
    left = pl.BlockSpec((length, BLOCK), lambda r, place: (0, place[r]))
    half = BLOCK // 2

    lanes = 3 * columns + LANES
    return kernel_call(
        mixer_grad_kernel,
        "mixer_grads",
        [jax.ShapeDtypeStruct((pairs, half, lanes), BF16)] * 2
        + [jax.ShapeDtypeStruct((width, LANES), F32)],
        flops=6 * length * width * columns,
        moved=8 * length * width,
        grid_spec=pltpu.PrefetchScalarGridSpec(
            num_scalar_prefetch=1,
            grid=(pairs,),
            in_specs=[
                left,
                all_at((length, 2 * columns)),
                left,
                all_at((length, columns)),
                pl.BlockSpec((BLOCK, 2 * columns), lambda r, place: (place[r], 0)),
                all_at((2, slots, BLOCK, BLOCK)),
            ],
            out_specs=[pl.BlockSpec((1, half, lanes), lambda r, place: (r, 0, 0))] * 2
            + [pl.BlockSpec((BLOCK, LANES), lambda r, place: (place[r], 0))],
        ),
    )


def same(arrays):
    return [jax.ShapeDtypeStruct(a.shape, F32) for a in arrays]


def on_device(
    tokens,
    cotangent,
    start_state,
    slot_table,
    norm_gains,
    gain_first,
    gain_second,
    block_params,
    block_first,
    block_second,
    input_weights,
    input_first,
    input_second,
    output_weights,
    output_first,
    output_second,
    gate_weights,
    gate_first,
    gate_second,
    hidden_weights,
    hidden_first,
    hidden_second,
    down_weights,
    down_first,
    down_second,
):
    slots = slot_table.shape[0]
    columns = slots * BLOCK
    ff = hidden_weights.shape[2]
    chunk, width = tokens.shape
    length = GROUP * chunk
    share = input_weights.shape[1]
    mixer, find_factors, unmixer = recurrence_calls(chunk, slots, width, share)
    pull, feed, push_down, feed_grads = feed_calls(length, width, share, ff)
    mixer_grads = mixer_grad_call(length, width, columns, slots)

    z, x = lax.axis_index("z"), lax.axis_index("x")
    h, y, core = lax.axis_index("h"), lax.axis_index("y"), lax.axis_index("c")
    chunks = jnp.arange(GROUP, dtype=jnp.int32)
    order = 2 * ((chunks // 2 - z + RING) % RING) + ((chunks % 2) ^ x)
    chunk_of = 2 * ((chunks // 2 + z) % RING) + ((chunks % 2) ^ x)

    place = jnp.concatenate(
        [RING * (h ^ (chunks // RING)) + (y + chunks) % RING, core[None]]
    ).astype(jnp.int32)

    mixer_lines = kernel_call(
        mixer_rows_kernel, "mixer_rows", jax.ShapeDtypeStruct((share, 3 * columns + LANES), BF16)
    )(input_weights, output_weights, gate_weights)
    column_mask = jnp.repeat((slot_table >= 0).astype(F32), BLOCK)
    select = (slot_table[:, None] == jnp.arange(NBLK, dtype=jnp.int32)[None, :]).astype(F32)
    vectors = jnp.einsum("sb,bkc->ksc", select, block_params, precision=HIGHEST).reshape(
        KERNEL + 4, columns
    )
    pars = jnp.concatenate(
        [
            jax.nn.softplus(-vectors[:1]),
            vectors[1:],
            jax.nn.sigmoid(-vectors[:1]),
            column_mask[None],
            start_state,
            jnp.zeros((5, columns), F32),
        ],
        axis=0,
    )

    values = tokens.astype(F32)
    normed = gather(scale_norm(values, norm_gains[0]).astype(BF16))
    other, normed[1], normed[3], normed[9] = lax.optimization_barrier(
        (move(mixer_lines, "h", 1), normed[1], normed[3], normed[9])
    )
    given = gather_rows(mixer_lines, other, h)
    hidden_now, *normed = lax.optimization_barrier((hidden_weights, *normed))
    feed_lines = kernel_call(
        feed_rows_kernel, "feed_rows", jax.ShapeDtypeStruct((share, 3 * ff), BF16)
    )(hidden_now, down_weights)
    copies = jnp.broadcast_to(after(cotangent, *normed), (GROUP, chunk, width))
    pars, feed_lines, copies = lax.optimization_barrier((pars, feed_lines, copies))
    cotangents = trade(copies)
    other, given = lax.optimization_barrier((move(feed_lines, "h", 1), given))
    branch, states, mixed, part, normed_all, mixer_w = mixer(order, pars, given, *normed)
    feed_w = gather_rows(feed_lines, other, h)
    added, (factors, (d_hidden, cotangent_all)) = scatter(
        part,
        (
            find_factors(order, pars, mixer_w, branch, states),
            pull(order, cotangents, feed_w),
        ),
    )
    middle = values + added
    second = gather(scale_norm(middle, norm_gains[1]).astype(BF16))
    hidden, d_gate, d_up, part, second_all = feed(chunk_of, feed_w, d_hidden, *second)

    d_second, (feed_grad, lower) = scatter(
        part,
        (
            feed_grads(second_all, cotangent_all, d_gate, d_up, hidden),
            push_down(order, hidden, feed_w),
        ),
    )
    feed_part = scatter_rows(feed_grad)
    d_norm_two, inverse = norm_back(middle, norm_gains[1], d_second)
    gain_two = jnp.sum(d_second * middle * inverse, axis=0)
    d_middle = cotangent.astype(F32) + d_norm_two
    outs = gather(d_middle.astype(BF16))
    lower = trade(after(lower, *outs).reshape(GROUP, chunk, width))

    mixed = mixed.reshape(length, columns)
    d_branch, d_gates, d_vectors, part, out_all = unmixer(
        order, pars, mixer_w, mixer_w, mixer_w, branch, *factors, *outs
    )
    d_branch, feed_part = lax.optimization_barrier(
        (d_branch.reshape(length, 2 * columns), feed_part)
    )
    part, lower = lax.optimization_barrier((part, lower))
    pieces = trade(part.reshape(GROUP, chunk, width))
    mine, theirs, gain_one = mixer_grads(
        place, normed_all, d_branch, out_all, mixed, mixer_w, d_gates
    )
    mixer_share, mixer_other = scatter_seq(mine, theirs)
    feed_share, feed_other = halves(feed_part, h)
    gain_one = jnp.sum(gain_one, axis=1) / norm_gains[0]
    small = jnp.concatenate([gain_one, gain_two, d_vectors.reshape(-1)]).reshape(-1, LANES)
    small = sum_over(small, "cy")
    pieces, mixer_other, feed_other, small = lax.optimization_barrier(
        (pieces, mixer_other, feed_other, small)
    )
    d_normed = jnp.sum(pieces.astype(F32), axis=0)
    mixer_share = plus(mixer_share, move(mixer_other, "h", 1))
    feed_share = plus(feed_share, move(feed_other, "h", 1))
    layer_output = (middle + jnp.sum(lower.astype(F32), axis=0)).astype(BF16)
    d_norm_one, _ = norm_back(values, norm_gains[0], d_normed)
    tokens_gradient = d_middle + d_norm_one

    small = sum_over(small, "h").reshape(-1)
    block_terms = jnp.einsum(
        "sb,ksc->bkc",
        select,
        small[2 * width :].reshape(KERNEL + 4, slots, BLOCK),
        precision=HIGHEST,
    )
    small = sum_over(
        jnp.concatenate([small[: 2 * width], block_terms.reshape(-1)]).reshape(-1, LANES), "xz"
    ).reshape(-1)
    gain_grad = small[: 2 * width].reshape(2, width)
    block_grad = small[2 * width :].reshape(block_params.shape)

    feed_arrays = (
        hidden_weights, hidden_first, hidden_second, down_weights, down_first, down_second
    )
    feed_new = kernel_call(feed_adam_kernel, "feed_adam", same(feed_arrays), moved=1 << 23)(
        feed_share, *feed_arrays
    )
    mixer_arrays = (
        input_weights, input_first, input_second,
        output_weights, output_first, output_second,
        gate_weights, gate_first, gate_second,
    )
    mixer_new = kernel_call(mixer_adam_kernel, "mixer_adam", same(mixer_arrays), moved=1 << 23)(
        mixer_share, *mixer_arrays
    )
    return (
        layer_output,
        tokens_gradient,
        *adamw(norm_gains, gain_grad, gain_first, gain_second, SMALL_RATE, 0.0),
        *adamw(block_params, block_grad, block_first, block_second, VECTOR_RATE, 0.0),
        *mixer_new,
        *feed_new,
    )


def solution(mesh):
    seq, gate = ("h", "y", "c"), ("z", "x")
    split_mesh = jax.sharding.Mesh(mesh.devices.reshape(2, RING, 2, RING, 2), seq + gate)
    rows = P(seq + gate, None)
    split = P(None, seq, gate)
    turned = P(gate, seq)
    blocks = P(None, gate, seq, None)
    weights = (split,) * 3 + (turned,) * 3 + (blocks,) * 3 + (split,) * 3 + (turned,) * 3
    return jax.shard_map(
        on_device,
        mesh=split_mesh,
        in_specs=(rows, rows, P(seq, gate), P(gate)) + (P(),) * 6 + weights,
        out_specs=(rows, rows) + (P(),) * 6 + weights,
        check_vma=False,
    )
```
